1024 devices in a mesh: node: 32 (over z), local: 32 (over x, y, core).
Axes of the slice: x: 4, y: 4, z: 32, core: 2. Of those that a mesh axis runs over, the one named last changes fastest.
Arguments:
- out_grad: bfloat16 [512, 7168], P('node', 'local'), may hold values from -6 to 6
- groups: int32 [512, 4], P('node'), may hold values from 0 to 31, as said below
- route_weight: float32 [512, 4], P('node'), may hold values from 0.05 to 0.6
- saved_input: bfloat16 [4096, 7168], P('node'), may hold values from -6 to 6
- w_gate: bfloat16 [7168, 65536], P(None, ('node', 'local')), may hold values from -0.3125 to 0.3125
- w_up: bfloat16 [7168, 65536], P(None, ('node', 'local')), may hold values from -0.3125 to 0.3125
- w_down: bfloat16 [65536, 7168], P(('node', 'local')), may hold values from -0.0625 to 0.0625
Outputs:
- in_grad: bfloat16 [512, 7168], P('node', 'local')
- score_grad: float32 [512, 4], P('node')
The draws below stay inside these ranges and needn't reach their ends.
Inputs may be any that keep to these rules, and one draw needn't show every extreme that they name: Each token names 4 different node groups. Of the tokens of one node group, at most 4 name any one node group; in every draw some node group is named by exactly 4 tokens of every node group.
All inputs are finite; a program needn't handle non-finite values.
Results may differ from the reference program's by a relative error of at most 0.022.
Values may be sent and summed in bfloat16 or wider, within the bound.
No kernel may reach another device: no remote copies, remote signals or barrier semaphores. Data moves between devices by JAX's collectives and lax.ppermute only.
A program may use at most 32 MiB of HBM per device.

```python
import math
import jax
import jax.numpy as jnp
from jax import lax

D = 7168
FF = 2048
EXP_NODE = 1
GROUP_MOST = 4
TOK_NODE = 16
TOPK = 4
EXPERTS = 32
CAP = 4
ROWS = 128
TOKENS = 512
N_NODE = 32
N_LOCAL = 32


def node_table(key, common):
    hot_count = max(1, N_NODE // 8)
    order = jax.random.permutation(jax.random.fold_in(key, 1), N_NODE).astype(jnp.int32)
    where_common = jnp.argmax(order == common)
    order = order.at[where_common].set(order[0]).at[0].set(common)
    ranking = jnp.arange(N_NODE, dtype=jnp.int32)
    remaining = GROUP_MOST * TOK_NODE - hot_count * CAP
    cold_count = N_NODE - hot_count
    extra = (ranking - hot_count < remaining % cold_count).astype(jnp.int32)
    counts = jnp.where(ranking < hot_count, CAP, remaining // cold_count + extra)
    boundary = jnp.cumsum(counts)
    position = jnp.arange(GROUP_MOST * TOK_NODE, dtype=jnp.int32)
    rank_at = jnp.sum((position[:, None] >= boundary[None, :]).astype(jnp.int32), axis=1)
    labels = order[rank_at]
    route_table = labels.reshape(GROUP_MOST, TOK_NODE).T
    shuffle = jax.random.permutation(jax.random.fold_in(key, 2), TOK_NODE)
    return route_table[shuffle]


def draw_groups(key, part):
    key = jax.random.fold_in(key, 11)
    common = jax.random.randint(jax.random.fold_in(key, 1), (), 0, N_NODE).astype(jnp.int32)

    def node_key(node_index):
        return jax.random.fold_in(key, node_index + 100)
    node_keys = jax.vmap(node_key)(jnp.arange(N_NODE, dtype=jnp.int32))

    def table_of(sub_key):
        return node_table(sub_key, common)
    return jax.vmap(table_of)(node_keys).reshape(TOKENS, GROUP_MOST).astype(jnp.int32)


def spiked(drawn, stream_key, source, target, parts, factor):
    def block_of(dim):
        return (jnp.arange(drawn.shape[dim]) // (drawn.shape[dim] // parts)).reshape((-1,) + (1,) * (drawn.ndim - 1 - dim))

    first = jax.random.permutation(stream_key, parts)[block_of(target)]
    second = (block_of(target) + parts // 2) % parts
    return jnp.where((block_of(source) == first) | (block_of(source) == second), factor * drawn, drawn)


def level_of(stream_key, shape, split, least, top_value):
    def one(axis_at, shards_of):
        heights = jax.random.uniform(jax.random.fold_in(jax.random.fold_in(stream_key, 6), axis_at), (shards_of,), jnp.float32, least / len(split), top_value / len(split))
        return jnp.repeat(jnp.exp(heights), shape[axis_at] // shards_of).reshape((-1,) + (1,) * (len(shape) - axis_at - 1))

    factor_of = one(*split[0])
    for cut in split[1:]:
        factor_of = factor_of * one(*cut)
    return factor_of


def normal_values(stream_key, shape, width, limit, shards=(), kind=jnp.bfloat16):
    loudness = level_of(stream_key, shape, shards, -0.22, 0.18) if shards else 1.0
    array = jax.random.normal(stream_key, shape, jnp.float32) * width * loudness
    return jnp.minimum(jnp.maximum(array, -limit), limit).astype(kind)


def noise_with(rng, dims, spread, bound, split, heavy, kind=jnp.bfloat16):
    array = spread * jax.random.normal(rng, dims, jnp.float32)
    if split:
        array = array * level_of(rng, dims, split, -0.22, 0.18)
    return jnp.clip(spiked(array, jax.random.fold_in(rng, 3), *heavy), -bound, bound).astype(kind)


def setup_inputs(seed: int = 0) -> dict:
    seeds = jax.random.split(jax.random.key(seed), 8)
    return {
        "out_grad": normal_values(seeds[0], (TOKENS, D), 1.0, 6.0, ((0, 32), (1, 32))),
        "groups": draw_groups(jax.random.fold_in(seeds[7], 71), 0),
        "route_weight": jnp.clip(jnp.exp(math.log(0.6) - 2.4849067 * jax.random.uniform(seeds[2], (TOKENS, TOPK), jnp.float32) ** level_of(seeds[2], (TOKENS, TOPK), ((0, 32),), -0.2, 0.2)), 0.05, 0.6),
        "saved_input": normal_values(seeds[3], (N_NODE * ROWS, D), 1.0, 6.0, ((0, 32),)),
        "w_gate": noise_with(seeds[4], (D, EXPERTS * FF), D ** -0.5, 0.3125, ((1, 1024),), (1, 0, 1024, 6.0)),
        "w_up": noise_with(seeds[5], (D, EXPERTS * FF), D ** -0.5, 0.3125, ((1, 1024),), (1, 0, 1024, 6.0)),
        "w_down": normal_values(seeds[6], (EXPERTS * FF, D), D ** -0.5, 0.0625, ((0, 1024),)),
    }


HIGH = lax.Precision.HIGHEST


def visit_tables(groups):
    node_ids = jnp.arange(N_NODE, dtype=jnp.int32)
    chosen_int = (groups.reshape(N_NODE, TOK_NODE, GROUP_MOST)[..., None] == node_ids).astype(jnp.int32)
    visits = jnp.sum(chosen_int, axis=2)
    slot_rank = jnp.cumsum(visits, axis=1) - visits
    slot_ids = jnp.arange(CAP, dtype=jnp.int32)
    placement = visits[..., None] * (slot_rank[..., None] == slot_ids).astype(jnp.int32)
    return chosen_int.astype(jnp.float32), placement.astype(jnp.float32)


def reference(out_grad, groups, route_weight, saved_input, w_gate, w_up, w_down):
    chosen, placement = visit_tables(groups)
    rounded_scale = lax.optimization_barrier(route_weight.astype(jnp.bfloat16))
    route_scale = rounded_scale.astype(jnp.float32).reshape(N_NODE, TOK_NODE, GROUP_MOST, EXP_NODE)
    node_scale = jnp.einsum('ntij,ntie->ntje', chosen, route_scale, precision=HIGH)
    token_grads = out_grad.astype(jnp.float32).reshape(N_NODE, TOK_NODE, D)
    arriving = jnp.einsum('ntjc,ntd->jncd', placement, token_grads, precision=HIGH)
    arriving = arriving.astype(jnp.bfloat16).reshape(N_NODE, ROWS, D)
    arriving_scale = jnp.einsum('ntjc,ntje->jnce', placement, node_scale, precision=HIGH)
    arriving_scale = arriving_scale.reshape(N_NODE, ROWS, EXP_NODE)
    inputs = saved_input.reshape(N_NODE, ROWS, D)
    node_cols = EXP_NODE * FF
    block_cols = node_cols // N_LOCAL

    def one_node(operands):
        node_index, rows_in, rows_grad, rows_scale = operands
        gate_cols = lax.dynamic_slice_in_dim(w_gate, node_index * node_cols, node_cols, 1)
        up_cols = lax.dynamic_slice_in_dim(w_up, node_index * node_cols, node_cols, 1)
        down_rows = lax.dynamic_slice_in_dim(w_down, node_index * node_cols, node_cols, 0)
        gate_pre = jnp.dot(rows_in, gate_cols, preferred_element_type=jnp.float32)
        up_pre = jnp.dot(rows_in, up_cols, preferred_element_type=jnp.float32)
        down_grad = lax.dot_general(rows_grad, down_rows, (((1,), (1,)), ((), ())), preferred_element_type=jnp.float32)
        sigmoid_gate = jax.nn.sigmoid(gate_pre)
        silu_value = gate_pre * sigmoid_gate
        activation = silu_value * up_pre
        row_score = jnp.sum((activation * down_grad).reshape(ROWS, EXP_NODE, FF), axis=2)
        hidden_grad = jnp.repeat(rows_scale, FF, axis=1) * down_grad
        gate_grad = (hidden_grad * up_pre * sigmoid_gate * (1.0 + gate_pre * (1.0 - sigmoid_gate))).astype(jnp.bfloat16)
        up_grad = (hidden_grad * silu_value).astype(jnp.bfloat16)

        def add_block(running, block_index):
            offset = block_index * block_cols
            gate_part = lax.dynamic_slice_in_dim(gate_grad, offset, block_cols, 1)
            up_part = lax.dynamic_slice_in_dim(up_grad, offset, block_cols, 1)
            gate_block = lax.dynamic_slice_in_dim(gate_cols, offset, block_cols, 1)
            up_block = lax.dynamic_slice_in_dim(up_cols, offset, block_cols, 1)
            term = lax.dot_general(gate_part, gate_block, (((1,), (1,)), ((), ())), preferred_element_type=jnp.float32)
            term = term + lax.dot_general(up_part, up_block, (((1,), (1,)), ((), ())), preferred_element_type=jnp.float32)
            rounded = lax.optimization_barrier(term.astype(jnp.bfloat16))
            return running + rounded.astype(jnp.float32), None

        row_part = lax.scan(add_block, jnp.zeros((ROWS, D), jnp.float32), jnp.arange(N_LOCAL, dtype=jnp.int32))[0]
        return row_part, row_score

    row_part, row_score = lax.map(one_node, (jnp.arange(N_NODE, dtype=jnp.int32), inputs, arriving, arriving_scale))
    returned = row_part.reshape(N_NODE, N_NODE, CAP, D)
    in_grad = jnp.einsum('ntjc,jncd->ntd', placement, returned, precision=HIGH)
    in_grad = in_grad.astype(jnp.bfloat16).reshape(TOKENS, D)
    score_back = row_score.reshape(N_NODE, N_NODE, CAP, EXP_NODE)
    values = jnp.einsum('ntjc,jnce->ntje', placement, score_back, precision=HIGH)
    score_grad = jnp.einsum('ntij,ntje->ntie', chosen, values, precision=HIGH).reshape(TOKENS, TOPK)
    return in_grad, score_grad
```

```python
import jax
import jax.numpy as jnp
from jax import lax
from jax.experimental import pallas as pl
from jax.experimental.pallas import tpu as pltpu
from jax.sharding import PartitionSpec as P

GROUP_MOST = 4
CAP = 4
LANES = 128
BF16 = jnp.bfloat16
F32 = jnp.float32
ROW_PAD = 240


def dot(a, b, contract):
    return lax.dot_general(
        a, b, ((contract[:1], contract[1:]), ((), ())), preferred_element_type=F32
    )


def iota(shape, dim):
    return lax.broadcasted_iota(jnp.int32, shape, dim)


def send_kernel(grad_ref, groups_ref, weight_ref, send_ref, place_ref):
    tokens, width = grad_ref.shape
    rows = send_ref.shape[0]
    row = iota((rows, tokens), 0)
    node, half, slot = row // (2 * CAP), row // CAP % 2, row % CAP
    named = [(groups_ref[i : i + 1, :] == node).astype(F32) for i in range(GROUP_MOST)]
    visits = named[0] + named[1] + named[2] + named[3]
    before = (iota((tokens, tokens), 0) < iota((tokens, tokens), 1)).astype(BF16)
    rank = dot(visits.astype(BF16), before, (1, 0))
    here = (rank == slot.astype(F32)).astype(F32)
    rounded = weight_ref[...].astype(BF16).astype(F32)
    scale = jnp.zeros((rows, tokens), F32)
    for i in range(GROUP_MOST):
        scale = scale + named[i] * rounded[i : i + 1, :]
    low = (half == 0).astype(F32) * here
    high = (half == 1).astype(F32) * here
    grad = grad_ref[...]
    rest = width - LANES
    grad_high = jnp.concatenate(
        [grad[:, LANES:].astype(F32), jnp.zeros((tokens, LANES - rest), F32)], axis=1
    ).astype(BF16)
    total = dot((low * visits).astype(BF16), grad[:, :LANES], (1, 0))
    total = total + dot((high * visits).astype(BF16), grad_high, (1, 0))
    row_scale = jnp.sum(high * scale, axis=1, keepdims=True)
    total = total + jnp.where(iota(total.shape, 1) == rest, row_scale, 0.0)
    send_ref[...] = total.astype(BF16)
    parts = [(part * named[i]) for part in (low, high) for i in range(GROUP_MOST)]
    place_ref[...] = jnp.concatenate(parts, axis=1).astype(BF16)


def pick(half, rows, arrivals):
    row, arrival = iota((rows, arrivals), 0), iota((rows, arrivals), 1)
    same = (row // (2 * CAP) == arrival // CAP) & (row % CAP == arrival % CAP)
    return (same & (row // CAP % 2 == half)).astype(BF16)


def spread_kernel(recv_ref, spread_ref, scale_ref):
    rows = recv_ref.shape[0]
    copies, width, arrivals = spread_ref.shape
    recv = recv_ref[...]
    low = dot(recv, pick(0, rows, arrivals), (0, 0))
    high = dot(recv, pick(1, rows, arrivals), (0, 0))
    rest = width - LANES
    scale_ref[...] = high[rest : rest + 1, :]
    slab = jnp.concatenate([low, high[:rest, :]], axis=0).astype(BF16)
    for i in range(copies):
        spread_ref[i] = slab


def expert_kernel(rows_ref, down_ref, gate_pre_ref, up_pre_ref, scale_ref, gate_ref, up_ref, term_ref):
    down_grad = dot(down_ref[...], rows_ref[...], (1, 0))
    gate_pre, up_pre = gate_pre_ref[...], up_pre_ref[...]
    sigmoid_gate = jax.nn.sigmoid(gate_pre)
    silu_value = gate_pre * sigmoid_gate
    score = jnp.sum(silu_value * up_pre * down_grad, axis=0, keepdims=True)
    hidden_grad = scale_ref[...] * down_grad
    gate_grad = hidden_grad * up_pre * sigmoid_gate * (1.0 + gate_pre * (1.0 - sigmoid_gate))
    up_grad = hidden_grad * silu_value
    grads = jnp.concatenate([gate_grad, up_grad], axis=0).astype(BF16)
    holders, padded, arrivals = term_ref.shape
    width = gate_ref.shape[1] // holders
    piece = 32
    for tile in range(gate_ref.shape[1] // LANES):
        at = slice(tile * LANES, (tile + 1) * LANES)
        weights = jnp.concatenate([gate_ref[:, at], up_ref[:, at]], axis=0)
        term = dot(weights, grads, (0, 0)).astype(BF16)
        for k in range(LANES // piece):
            first = tile * LANES + k * piece
            holder, offset = first // width, first % width
            term_ref[holder, offset : offset + piece, :] = term[k * piece : (k + 1) * piece]
    score_high = score.astype(BF16).astype(F32)
    extra_row = iota((padded - width, arrivals), 0)
    extra = jnp.where(extra_row == 0, score_high, jnp.where(extra_row == 1, score - score_high, 0.0))
    extra = extra.astype(BF16)
    for holder in range(holders):
        term_ref[holder, width:padded, :] = extra


def return_kernel(width, part_ref, back_ref):
    holders, padded, arrivals = part_ref.shape
    total = part_ref[0].astype(F32)
    for holder in range(1, holders):
        total = total + part_ref[holder].astype(F32)
    rows = back_ref.shape[0]
    score = total[width : width + 1, :] + total[width + 1 : width + 2, :]
    score_high = score.astype(BF16).astype(F32)
    extra_row = iota((2 * LANES - width, arrivals), 0)
    extra = jnp.where(extra_row == 0, score_high, jnp.where(extra_row == 1, score - score_high, 0.0))
    low = total[:LANES].astype(BF16)
    high = jnp.concatenate([total[LANES:width], extra], axis=0).astype(BF16)
    back = dot(pick(0, rows, arrivals), low, (1, 1)) + dot(pick(1, rows, arrivals), high, (1, 1))
    back_ref[...] = back.astype(BF16)


def combine_kernel(back_ref, place_ref, grad_ref, score_ref):
    tokens, width = grad_ref.shape
    rest = width - LANES
    back, place = back_ref[...], place_ref[...]
    sums = dot(place, back, (0, 0))
    low = sums[0:tokens]
    high = sums[GROUP_MOST * tokens : (GROUP_MOST + 1) * tokens]
    for i in range(1, GROUP_MOST):
        low = low + sums[i * tokens : (i + 1) * tokens]
        high = high + sums[(GROUP_MOST + i) * tokens : (GROUP_MOST + i + 1) * tokens]
    grad_ref[:, :LANES] = low.astype(BF16)
    grad_ref[:, LANES:] = high[:, :rest].astype(BF16)
    lane = iota((16, LANES), 1)
    chosen = (lane == rest + iota((16, LANES), 0)) & (iota((16, LANES), 0) < 2)
    scores = dot(chosen.astype(BF16), back, (1, 1)).astype(BF16)
    values = dot(scores, place, (1, 0))
    values = values[0:1] + values[1:2]
    for i in range(GROUP_MOST):
        first = (GROUP_MOST + i) * tokens
        score_ref[i : i + 1, :] = values[:, first : first + tokens]


def shape(dims, dtype):
    return jax.ShapeDtypeStruct(dims, dtype)


def on_device(out_grad, groups, route_weight, saved_input, w_gate, w_up, w_down):
    tokens, width = out_grad.shape
    nodes, holders = lax.axis_size("node"), lax.axis_size("local")
    rows, arrivals = nodes * 2 * CAP, nodes * CAP
    send, place = pl.pallas_call(
        send_kernel, out_shape=(shape((rows, LANES), BF16), shape((rows, LANES), BF16))
    )(out_grad, groups.T, route_weight.T)
    recv = lax.all_to_all(
        send.reshape(nodes, 2 * CAP, LANES), "node", split_axis=0, concat_axis=0, tiled=True
    ).reshape(rows, LANES)
    gate_pre = lax.dot_general(
        w_gate, saved_input, (((0,), (1,)), ((), ())), preferred_element_type=F32
    )
    up_pre = lax.dot_general(
        w_up, saved_input, (((0,), (1,)), ((), ())), preferred_element_type=F32
    )
    spread, scale = pl.pallas_call(
        spread_kernel, out_shape=(shape((holders, width, arrivals), BF16), shape((1, arrivals), F32))
    )(recv)
    full = lax.all_to_all(spread, "local", split_axis=0, concat_axis=0, tiled=True)
    term = pl.pallas_call(
        expert_kernel,
        out_shape=shape((holders, ROW_PAD, arrivals), BF16),
        compiler_params=pltpu.CompilerParams(vmem_limit_bytes=32 * 1024 * 1024),
    )(full.reshape(-1, arrivals), w_down, gate_pre, up_pre, scale, w_gate.T, w_up.T)
    part = lax.all_to_all(term, "local", split_axis=0, concat_axis=0, tiled=True)
    back = pl.pallas_call(
        lambda *refs: return_kernel(width, *refs), out_shape=shape((rows, LANES), BF16)
    )(part)
    back = lax.all_to_all(
        back.reshape(nodes, 2 * CAP, LANES), "node", split_axis=0, concat_axis=0, tiled=True
    ).reshape(rows, LANES)
    in_grad, score = pl.pallas_call(
        combine_kernel, out_shape=(shape((tokens, width), BF16), shape((GROUP_MOST, tokens), F32))
    )(back, place)
    return in_grad, score.T


def solution(mesh):
    placed = (
        P("node", "local"),
        P("node", None),
        P("node", None),
        P("node", None),
        P(None, ("node", "local")),
        P(None, ("node", "local")),
        P(("node", "local"), None),
    )
    return jax.shard_map(
        on_device,
        mesh=mesh,
        in_specs=placed,
        out_specs=(P("node", "local"), P("node", None)),
        check_vma=False,
    )
```

```python
import jax
import jax.numpy as jnp
from jax import lax
from jax.experimental import pallas as pl
from jax.experimental.pallas import tpu as pltpu
from jax.sharding import PartitionSpec as P

GROUP_MOST = 4
CAP = 4
LANES = 128
BF16 = jnp.bfloat16
F32 = jnp.float32
ROW_PAD = 240


def dot(a, b, contract):
    return lax.dot_general(
        a, b, ((contract[:1], contract[1:]), ((), ())), preferred_element_type=F32
    )


def iota(shape, dim):
    return lax.broadcasted_iota(jnp.int32, shape, dim)


def chip_at(position, chips):
    return (position + 5 * chips // 8) % chips


def node_of(row, nodes):
    return (row // (2 * CAP) + nodes // 2) % nodes


def fetch(pairs, sems):
    copies = [pltpu.make_async_copy(src, dst, sems.at[i]) for i, (src, dst) in enumerate(pairs)]
    for copy in copies:
        copy.start()
    return copies


def placement(groups, rows):
    tokens = groups.shape[1]
    row = iota((tokens, rows), 1)
    node, half, slot = node_of(row, rows // (2 * CAP)), row // CAP % 2, row % CAP
    same = (iota((tokens, tokens), 0) == iota((tokens, tokens), 1)).astype(BF16)
    columns = dot(same, groups.astype(F32).astype(BF16), (1, 1)).astype(jnp.int32)
    named = [(columns[:, i : i + 1] == node).astype(F32) for i in range(GROUP_MOST)]
    visits = named[0] + named[1] + named[2] + named[3]
    earlier = (iota((tokens, tokens), 1) < iota((tokens, tokens), 0)).astype(BF16)
    rank = dot(earlier, visits.astype(BF16), (1, 0))
    here = (rank == slot.astype(F32)).astype(F32)
    return named, visits, here * (half == 0).astype(F32), here * (half == 1).astype(F32)


def send_kernel(grad_hbm, groups_hbm, weight_hbm, send_ref, grad_ref, groups_ref, weight_ref, sems):
    tokens, width = grad_ref.shape
    rows = send_ref.shape[0]
    rest = width - LANES
    copies = fetch(
        [(groups_hbm, groups_ref), (weight_hbm, weight_ref), (grad_hbm, grad_ref)], sems
    )
    copies[0].wait()
    named, visits, low, high = placement(groups_ref[...], rows)
    copies[1].wait()
    same = (iota((tokens, tokens), 0) == iota((tokens, tokens), 1)).astype(BF16)
    columns = dot(same, weight_ref[...].astype(BF16), (1, 1))
    scale = columns[:, 0:1] * named[0]
    for i in range(1, GROUP_MOST):
        scale = scale + columns[:, i : i + 1] * named[i]
    picks = jnp.concatenate([low * visits, high * visits, high * scale], axis=0).astype(BF16)
    copies[2].wait()
    grad = grad_ref[...].astype(F32)
    values = jnp.concatenate(
        [
            grad[:, :LANES],
            jnp.concatenate([grad[:, LANES:], jnp.zeros((tokens, LANES - rest), F32)], axis=1),
            (iota((tokens, LANES), 1) == rest).astype(F32),
        ],
        axis=0,
    ).astype(BF16)
    send_ref[...] = dot(picks, values, (0, 0)).astype(BF16)


def pick(half, rows, arrivals):
    row, arrival = iota((rows, arrivals), 0), iota((rows, arrivals), 1)
    same = (node_of(row, rows // (2 * CAP)) == arrival // CAP) & (row % CAP == arrival % CAP)
    return (same & (row // CAP % 2 == half)).astype(BF16)


def spread_kernel(recv_ref, spread_hbm, scale_ref, slab_ref, sems):
    rows = recv_ref.shape[0]
    width, arrivals = slab_ref.shape
    recv = recv_ref[...]
    low = dot(recv, pick(0, rows, arrivals), (0, 0))
    high = dot(recv, pick(1, rows, arrivals), (0, 0))
    rest = width - LANES
    scale_ref[...] = high[rest : rest + 1, :]
    slab_ref[...] = jnp.concatenate([low, high[:rest, :]], axis=0).astype(BF16)
    copies = fetch([(slab_ref, spread_hbm.at[i]) for i in range(spread_hbm.shape[0])], sems)
    for copy in copies:
        copy.wait()


def prepare_down_kernel(down_ref, down_pair_ref, prepared_ref, down_part_ref):
    units = down_ref.shape[0]
    chips, _, width = down_part_ref.shape
    core = lax.axis_index("core")
    for parity in range(2):

        @pl.when(core == parity)
        def _():
            for k in range(chips):
                first = (2 * chip_at(k, chips) + parity) * width
                down_part_ref[k, :units] = down_ref[:, first : first + width]
                down_part_ref[k, units:] = down_pair_ref[:, first : first + width]


def prepare_kernel(
    saved_hbm, gate_hbm, gate_pair_hbm, up_hbm, up_pair_hbm, groups_ref,
    pre_ref, back_part_ref, place_ref,
    saved_ref, weight_ref, sems,
):
    units = gate_hbm.shape[0]
    chips, width, _ = back_part_ref.shape
    copies = fetch(
        [
            (gate_hbm, weight_ref.at[pl.ds(0, units)]),
            (gate_pair_hbm, weight_ref.at[pl.ds(units, units)]),
            (up_hbm, weight_ref.at[pl.ds(2 * units, units)]),
            (up_pair_hbm, weight_ref.at[pl.ds(3 * units, units)]),
            (saved_hbm, saved_ref),
        ],
        sems,
    )
    named, _, low, high = placement(groups_ref[...], place_ref.shape[1])
    parts = [part * named[i] for part in (low, high) for i in range(GROUP_MOST)]
    place_ref[...] = jnp.concatenate(parts, axis=0).astype(BF16)
    core = lax.axis_index("core")
    for copy in copies[:4]:
        copy.wait()
    for parity in range(2):

        @pl.when(core == parity)
        def _():
            for k in range(chips):
                first = (2 * chip_at(k, chips) + parity) * width
                back_part_ref[k] = weight_ref[:, first : first + width].T

    copies[4].wait()
    pre_ref[...] = dot(weight_ref[...], saved_ref[...], (1, 1))


def down_kernel(rows_ref, down_ref, part_ref):
    total = dot(down_ref[0], rows_ref[0], (1, 0))
    for k in range(1, rows_ref.shape[0]):
        total = total + dot(down_ref[k], rows_ref[k], (1, 0))
    part_ref[...] = total


def expert_kernel(part_ref, pair_ref, pre_ref, scale_ref, weight_ref, term_ref):
    units = part_ref.shape[0] // 2
    pair = pair_ref[...]
    down_grad = part_ref[...] + jnp.concatenate([pair[units:], pair[:units]], axis=0)
    gate_pre, up_pre = pre_ref[: 2 * units, :], pre_ref[2 * units :, :]
    sigmoid_gate = jax.nn.sigmoid(gate_pre)
    silu_value = gate_pre * sigmoid_gate
    score = jnp.sum(silu_value * up_pre * down_grad, axis=0, keepdims=True)
    hidden_grad = scale_ref[...] * down_grad
    gate_grad = hidden_grad * up_pre * sigmoid_gate * (1.0 + gate_pre * (1.0 - sigmoid_gate))
    up_grad = hidden_grad * silu_value
    grads = jnp.concatenate([gate_grad, up_grad], axis=0).astype(BF16)
    chips, padded, arrivals = term_ref.shape
    width = weight_ref.shape[1]
    score_high = score.astype(BF16).astype(F32)
    extra_row = iota((padded - width, arrivals), 0)
    extra = jnp.where(extra_row == 0, score_high, jnp.where(extra_row == 1, score - score_high, 0.0))
    extra = extra.astype(BF16)
    for k in range(chips):
        term_ref[k, :width, :] = dot(weight_ref[k], grads, (1, 0)).astype(BF16)
        term_ref[k, width:padded, :] = extra


def return_kernel(width, part_ref, back_ref):
    holders, padded, arrivals = part_ref.shape
    total = part_ref[0].astype(F32)
    for holder in range(1, holders):
        total = total + part_ref[holder].astype(F32)
    rows = back_ref.shape[0]
    score = total[width : width + 1, :] + total[width + 1 : width + 2, :]
    score_high = score.astype(BF16).astype(F32)
    extra_row = iota((2 * LANES - width, arrivals), 0)
    extra = jnp.where(extra_row == 0, score_high, jnp.where(extra_row == 1, score - score_high, 0.0))
    low = total[:LANES].astype(BF16)
    high = jnp.concatenate([total[LANES:width], extra], axis=0).astype(BF16)
    back = dot(pick(0, rows, arrivals), low, (1, 1)) + dot(pick(1, rows, arrivals), high, (1, 1))
    back_ref[...] = back.astype(BF16)


def combine_kernel(back_ref, place_ref, grad_ref, score_ref):
    tokens, width = grad_ref.shape
    rest = width - LANES
    back, place = back_ref[...], place_ref[...]
    sums = dot(place, back, (1, 0))
    low = sums[0:tokens]
    high = sums[GROUP_MOST * tokens : (GROUP_MOST + 1) * tokens]
    for i in range(1, GROUP_MOST):
        low = low + sums[i * tokens : (i + 1) * tokens]
        high = high + sums[(GROUP_MOST + i) * tokens : (GROUP_MOST + i + 1) * tokens]
    grad_ref[:, :LANES] = low.astype(BF16)
    grad_ref[:, LANES:] = high[:, :rest].astype(BF16)
    lane = iota((16, LANES), 1)
    chosen = (lane == rest + iota((16, LANES), 0)) & (iota((16, LANES), 0) < 2)
    scores = dot(chosen.astype(BF16), back, (1, 1)).astype(BF16)
    values = dot(scores, place, (1, 1))
    values = values[0:1] + values[1:2]
    for i in range(GROUP_MOST):
        first = (GROUP_MOST + i) * tokens
        score_ref[i : i + 1, :] = values[:, first : first + tokens]


def shape(dims, dtype):
    return jax.ShapeDtypeStruct(dims, dtype)


def exchange(x, axis, groups=None):
    return lax.all_to_all(
        x, axis, split_axis=0, concat_axis=0, tiled=True, axis_index_groups=groups
    )


def memory(mebibytes):
    return pltpu.CompilerParams(vmem_limit_bytes=mebibytes * 1024 * 1024)


def swap(x):
    return lax.ppermute(x, "core", [(0, 1), (1, 0)])


def on_device(out_grad, groups, route_weight, saved_input, w_gate, w_up, w_down):
    tokens, width = out_grad.shape
    nodes, chips = lax.axis_size("node"), lax.axis_size("chip")
    rows, arrivals, units = nodes * 2 * CAP, nodes * CAP, w_down.shape[0]
    ring = [[(i + nodes // 2) % nodes for i in range(nodes)]]
    plane = [[chip_at(i, chips) for i in range(chips)]]
    hbm, vmem = pl.BlockSpec(memory_space=pltpu.HBM), pl.BlockSpec(memory_space=pltpu.VMEM)
    send = pl.pallas_call(
        send_kernel,
        in_specs=[hbm] * 3,
        out_shape=shape((rows, LANES), BF16),
        scratch_shapes=[
            pltpu.VMEM((tokens, width), BF16),
            pltpu.VMEM((GROUP_MOST, tokens), jnp.int32),
            pltpu.VMEM((GROUP_MOST, tokens), F32),
            pltpu.SemaphoreType.DMA((3,)),
        ],
    )(out_grad, groups.T, route_weight.T)
    w_gate, w_up = w_gate.T, w_up.T
    gate_pair, up_pair, down_pair = swap(w_gate), swap(w_up), swap(w_down)
    recv = exchange(send.reshape(nodes, 2 * CAP, LANES), "node", ring).reshape(rows, LANES)
    spread, scale = pl.pallas_call(
        spread_kernel,
        out_specs=(hbm, vmem),
        out_shape=(shape((chips, width, arrivals), BF16), shape((1, arrivals), F32)),
        scratch_shapes=[pltpu.VMEM((width, arrivals), BF16), pltpu.SemaphoreType.DMA((chips,))],
        compiler_params=memory(6),
    )(recv)
    features = saved_input.shape[1]
    pre, back_part, place = pl.pallas_call(
        prepare_kernel,
        in_specs=[hbm] * 5 + [vmem],
        out_shape=(
            shape((4 * units, arrivals), F32),
            shape((chips, width, 4 * units), BF16),
            shape((2 * GROUP_MOST * tokens, rows), BF16),
        ),
        scratch_shapes=[
            pltpu.VMEM((arrivals, features), BF16),
            pltpu.VMEM((4 * units, features), BF16),
            pltpu.SemaphoreType.DMA((5,)),
        ],
        compiler_params=memory(60),
        cost_estimate=pl.CostEstimate(
            flops=8 * units * arrivals * features, bytes_accessed=9 * 1024 * 1024, transcendentals=0
        ),
    )(saved_input, w_gate, gate_pair, w_up, up_pair, groups.T)
    down_part = pl.pallas_call(
        prepare_down_kernel,
        in_specs=[vmem, vmem, pl.BlockSpec(memory_space=pl.ANY)],
        out_shape=shape((chips, 2 * units, width), BF16),
        compiler_params=memory(6),
        cost_estimate=pl.CostEstimate(flops=0, bytes_accessed=4 * 1024 * 1024, transcendentals=0),
    )(w_down, down_pair, place)
    full = exchange(spread, "chip", plane)
    part = pl.pallas_call(
        down_kernel,
        out_shape=shape((2 * units, arrivals), F32),
        compiler_params=memory(6),
    )(full, down_part)
    pair = swap(part)
    term = pl.pallas_call(
        expert_kernel,
        out_shape=shape((chips, ROW_PAD, arrivals), BF16),
        compiler_params=memory(8),
    )(part, pair, pre, scale, back_part)
    terms = exchange(term, "chip", plane)
    back = pl.pallas_call(
        lambda *refs: return_kernel(width, *refs),
        out_shape=shape((rows, LANES), BF16),
        compiler_params=memory(6),
    )(terms)
    back = exchange(back.reshape(nodes, 2 * CAP, LANES), "node", ring).reshape(rows, LANES)
    in_grad, score = pl.pallas_call(
        combine_kernel,
        out_shape=(shape((tokens, width), BF16), shape((GROUP_MOST, tokens), F32)),
        compiler_params=memory(4),
    )(back, place)
    return in_grad, score.T


def solution(mesh):
    devices = mesh.devices
    split = jax.sharding.Mesh(
        devices.reshape(devices.shape[0], devices.shape[1] // 2, 2), ("node", "chip", "core")
    )
    local = ("chip", "core")
    every = ("node", "chip", "core")
    placed = (
        P("node", local),
        P("node", None),
        P("node", None),
        P("node", None),
        P(None, every),
        P(None, every),
        P(every, None),
    )
    return jax.shard_map(
        on_device,
        mesh=split,
        in_specs=placed,
        out_specs=(P("node", local), P("node", None)),
        check_vma=False,
    )
```

```python
import jax
import jax.numpy as jnp
from jax import lax
from jax.experimental import pallas as pl
from jax.experimental.pallas import tpu as pltpu
from jax.sharding import PartitionSpec as P

GROUP_MOST = 4
FIRST_OUT, FIRST_BACK = 20, 16
CAP = 4
LANES = 128
BF16 = jnp.bfloat16
F32 = jnp.float32
ROW_PAD = 240


def dot(a, b, contract):
    return lax.dot_general(
        a, b, ((contract[:1], contract[1:]), ((), ())), preferred_element_type=F32
    )


def iota(shape, dim):
    return lax.broadcasted_iota(jnp.int32, shape, dim)


def chip_at(position, chips):
    return (position + 5 * chips // 8) % chips


def node_at(position, nodes, first):
    return (position + first * nodes // 32) % nodes


def fetch(pairs, sems):
    copies = [pltpu.make_async_copy(src, dst, sems.at[i]) for i, (src, dst) in enumerate(pairs)]
    for copy in copies:
        copy.start()
    return copies


def placement(tokens, rows, first):
    row = iota((tokens, rows), 1)
    nodes = rows // (2 * CAP)
    node = node_at(row // (2 * CAP), nodes, first).astype(F32)
    half, slot = row // CAP % 2, (row % CAP).astype(F32)
    low, high = (half == 0).astype(F32), (half == 1).astype(F32)
    earlier = (iota((tokens, tokens), 1) < iota((tokens, tokens), 0)).astype(BF16)

    def of(columns):
        named = [(columns[:, i : i + 1] == node).astype(F32) for i in range(GROUP_MOST)]
        visits = named[0] + named[1] + named[2] + named[3]
        here = (dot(earlier, visits.astype(BF16), (1, 0)) == slot).astype(F32)
        return named, visits, here * low, here * high

    return of


def send_kernel(grad_hbm, groups_hbm, weight_hbm, send_ref, grad_ref, groups_ref, weight_ref, sems):
    tokens, width = grad_ref.shape
    rows = send_ref.shape[0]
    rest = width - LANES
    copies = fetch(
        [(groups_hbm, groups_ref), (weight_hbm, weight_ref), (grad_hbm, grad_ref)], sems
    )
    place = placement(tokens, rows, FIRST_OUT)
    same = (iota((tokens, tokens), 0) == iota((tokens, tokens), 1)).astype(BF16)
    marks = (iota((tokens, LANES), 1) == rest).astype(F32)
    copies[0].wait()
    copies[1].wait()
    both = jnp.concatenate([groups_ref[...].astype(F32), weight_ref[...]], axis=0)
    columns = dot(same, both.astype(BF16), (1, 1))
    named, visits, low, high = place(columns)
    scale = columns[:, GROUP_MOST : GROUP_MOST + 1] * named[0]
    for i in range(1, GROUP_MOST):
        scale = scale + columns[:, GROUP_MOST + i : GROUP_MOST + i + 1] * named[i]
    picks = jnp.concatenate([low * visits, high * visits, high * scale], axis=0).astype(BF16)
    copies[2].wait()
    grad = grad_ref[...].astype(F32)
    values = jnp.concatenate(
        [
            grad[:, :LANES],
            jnp.concatenate([grad[:, LANES:], jnp.zeros((tokens, LANES - rest), F32)], axis=1),
            marks,
        ],
        axis=0,
    ).astype(BF16)
    send_ref[...] = dot(picks, values, (0, 0)).astype(BF16)


def pick(half, rows, arrivals, first):
    row, arrival = iota((rows, arrivals), 0), iota((rows, arrivals), 1)
    node = node_at(row // (2 * CAP), rows // (2 * CAP), first)
    same = (node == arrival // CAP) & (row % CAP == arrival % CAP)
    return (same & (row // CAP % 2 == half)).astype(BF16)


def spread_kernel(recv_ref, spread_hbm, scale_ref, slab_ref, sems):
    rows = recv_ref.shape[0]
    width, arrivals = slab_ref.shape
    recv = recv_ref[...]
    low = dot(recv, pick(0, rows, arrivals, FIRST_OUT), (0, 0))
    high = dot(recv, pick(1, rows, arrivals, FIRST_OUT), (0, 0))
    rest = width - LANES
    scale_ref[...] = high[rest : rest + 1, :]
    slab_ref[...] = jnp.concatenate([low, high[:rest, :]], axis=0).astype(BF16)
    copies = fetch([(slab_ref, spread_hbm.at[i]) for i in range(spread_hbm.shape[0])], sems)
    for copy in copies:
        copy.wait()


def prepare_down_kernel(down_ref, down_pair_ref, prepared_ref, down_part_ref):
    units = down_ref.shape[0]
    chips, _, width = down_part_ref.shape
    core = lax.axis_index("core")
    for parity in range(2):

        @pl.when(core == parity)
        def _():
            for k in range(chips):
                first = (2 * chip_at(k, chips) + parity) * width
                down_part_ref[k, :units] = down_ref[:, first : first + width]
                down_part_ref[k, units:] = down_pair_ref[:, first : first + width]


def prepare_kernel(
    saved_hbm, gate_hbm, gate_pair_hbm, up_hbm, up_pair_hbm, groups_ref,
    pre_ref, back_part_ref, place_ref,
    saved_ref, weight_ref, sems,
):
    units = gate_hbm.shape[0]
    chips, width, _ = back_part_ref.shape
    copies = fetch(
        [
            (gate_hbm, weight_ref.at[pl.ds(0, units)]),
            (gate_pair_hbm, weight_ref.at[pl.ds(units, units)]),
            (up_hbm, weight_ref.at[pl.ds(2 * units, units)]),
            (up_pair_hbm, weight_ref.at[pl.ds(3 * units, units)]),
            (saved_hbm, saved_ref),
        ],
        sems,
    )
    tokens = groups_ref.shape[1]
    same = (iota((tokens, tokens), 0) == iota((tokens, tokens), 1)).astype(BF16)
    columns = dot(same, groups_ref[...].astype(F32).astype(BF16), (1, 1))
    named, _, low, high = placement(tokens, place_ref.shape[1], FIRST_BACK)(columns)
    parts = [part * named[i] for part in (low, high) for i in range(GROUP_MOST)]
    place_ref[...] = jnp.concatenate(parts, axis=0).astype(BF16)
    core = lax.axis_index("core")
    for copy in copies[:4]:
        copy.wait()
    for parity in range(2):

        @pl.when(core == parity)
        def _():
            for k in range(chips):
                first = (2 * chip_at(k, chips) + parity) * width
                back_part_ref[k] = weight_ref[:, first : first + width].T

    copies[4].wait()
    pre_ref[...] = dot(weight_ref[...], saved_ref[...], (1, 1))


def down_kernel(rows_ref, down_ref, part_ref):
    total = dot(down_ref[0], rows_ref[0], (1, 0))
    for k in range(1, rows_ref.shape[0]):
        total = total + dot(down_ref[k], rows_ref[k], (1, 0))
    part_ref[...] = total


def expert_kernel(part_ref, pair_ref, pre_ref, scale_ref, weight_ref, term_ref):
    units = part_ref.shape[0] // 2
    pair = pair_ref[...]
    down_grad = part_ref[...] + jnp.concatenate([pair[units:], pair[:units]], axis=0)
    gate_pre, up_pre = pre_ref[: 2 * units, :], pre_ref[2 * units :, :]
    sigmoid_gate = jax.nn.sigmoid(gate_pre)
    silu_value = gate_pre * sigmoid_gate
    score = jnp.sum(silu_value * up_pre * down_grad, axis=0, keepdims=True)
    hidden_grad = scale_ref[...] * down_grad
    gate_grad = hidden_grad * up_pre * sigmoid_gate * (1.0 + gate_pre * (1.0 - sigmoid_gate))
    up_grad = hidden_grad * silu_value
    grads = jnp.concatenate([gate_grad, up_grad], axis=0).astype(BF16)
    chips, padded, arrivals = term_ref.shape
    width = weight_ref.shape[1]
    score_high = score.astype(BF16).astype(F32)
    extra_row = iota((padded - width, arrivals), 0)
    extra = jnp.where(extra_row == 0, score_high, jnp.where(extra_row == 1, score - score_high, 0.0))
    extra = extra.astype(BF16)
    for k in range(chips):
        term_ref[k, :width, :] = dot(weight_ref[k], grads, (1, 0)).astype(BF16)
        term_ref[k, width:padded, :] = extra


def return_kernel(width, part_ref, back_ref):
    holders, padded, arrivals = part_ref.shape
    total = part_ref[0].astype(F32)
    for holder in range(1, holders):
        total = total + part_ref[holder].astype(F32)
    rows = back_ref.shape[0]
    score = total[width : width + 1, :] + total[width + 1 : width + 2, :]
    score_high = score.astype(BF16).astype(F32)
    extra_row = iota((2 * LANES - width, arrivals), 0)
    extra = jnp.where(extra_row == 0, score_high, jnp.where(extra_row == 1, score - score_high, 0.0))
    low = total[:LANES].astype(BF16)
    high = jnp.concatenate([total[LANES:width], extra], axis=0).astype(BF16)
    back = dot(pick(0, rows, arrivals, FIRST_BACK), low, (1, 1))
    back = back + dot(pick(1, rows, arrivals, FIRST_BACK), high, (1, 1))
    back_ref[...] = back.astype(BF16)


def combine_kernel(back_ref, place_ref, grad_ref, score_ref):
    tokens, width = grad_ref.shape
    rest = width - LANES
    back, place = back_ref[...], place_ref[...]
    sums = dot(place, back, (1, 0))
    low = sums[0:tokens]
    high = sums[GROUP_MOST * tokens : (GROUP_MOST + 1) * tokens]
    for i in range(1, GROUP_MOST):
        low = low + sums[i * tokens : (i + 1) * tokens]
        high = high + sums[(GROUP_MOST + i) * tokens : (GROUP_MOST + i + 1) * tokens]
    grad_ref[:, :LANES] = low.astype(BF16)
    grad_ref[:, LANES:] = high[:, :rest].astype(BF16)
    lane = iota((16, LANES), 1)
    chosen = (lane == rest + iota((16, LANES), 0)) & (iota((16, LANES), 0) < 2)
    scores = dot(chosen.astype(BF16), back, (1, 1)).astype(BF16)
    values = dot(scores, place, (1, 1))
    values = values[0:1] + values[1:2]
    for i in range(GROUP_MOST):
        first = (GROUP_MOST + i) * tokens
        score_ref[i : i + 1, :] = values[:, first : first + tokens]


def shape(dims, dtype):
    return jax.ShapeDtypeStruct(dims, dtype)


def exchange(x, axis, groups=None):
    return lax.all_to_all(
        x, axis, split_axis=0, concat_axis=0, tiled=True, axis_index_groups=groups
    )


def memory(mebibytes):
    return pltpu.CompilerParams(vmem_limit_bytes=mebibytes * 1024 * 1024)


def swap(x):
    return lax.ppermute(x, "core", [(0, 1), (1, 0)])


def on_device(out_grad, groups, route_weight, saved_input, w_gate, w_up, w_down):
    tokens, width = out_grad.shape
    nodes, chips = lax.axis_size("node"), lax.axis_size("chip")
    rows, arrivals, units = nodes * 2 * CAP, nodes * CAP, w_down.shape[0]
    ring_out = [[node_at(i, nodes, FIRST_OUT) for i in range(nodes)]]
    ring_back = [[node_at(i, nodes, FIRST_BACK) for i in range(nodes)]]
    plane = [[chip_at(i, chips) for i in range(chips)]]
    hbm, vmem = pl.BlockSpec(memory_space=pltpu.HBM), pl.BlockSpec(memory_space=pltpu.VMEM)
    send = pl.pallas_call(
        send_kernel,
        in_specs=[hbm] * 3,
        out_shape=shape((rows, LANES), BF16),
        scratch_shapes=[
            pltpu.VMEM((tokens, width), BF16),
            pltpu.VMEM((GROUP_MOST, tokens), jnp.int32),
            pltpu.VMEM((GROUP_MOST, tokens), F32),
            pltpu.SemaphoreType.DMA((3,)),
        ],
    )(out_grad, groups.T, route_weight.T)
    w_gate, w_up = w_gate.T, w_up.T
    gate_pair, up_pair, down_pair = swap(w_gate), swap(w_up), swap(w_down)
    recv = exchange(send.reshape(nodes, 2 * CAP, LANES), "node", ring_out).reshape(rows, LANES)
    spread, scale = pl.pallas_call(
        spread_kernel,
        out_specs=(hbm, vmem),
        out_shape=(shape((chips, width, arrivals), BF16), shape((1, arrivals), F32)),
        scratch_shapes=[pltpu.VMEM((width, arrivals), BF16), pltpu.SemaphoreType.DMA((chips,))],
        compiler_params=memory(6),
    )(recv)
    features = saved_input.shape[1]
    pre, back_part, place = pl.pallas_call(
        prepare_kernel,
        in_specs=[hbm] * 5 + [vmem],
        out_shape=(
            shape((4 * units, arrivals), F32),
            shape((chips, width, 4 * units), BF16),
            shape((2 * GROUP_MOST * tokens, rows), BF16),
        ),
        scratch_shapes=[
            pltpu.VMEM((arrivals, features), BF16),
            pltpu.VMEM((4 * units, features), BF16),
            pltpu.SemaphoreType.DMA((5,)),
        ],
        compiler_params=memory(60),
        cost_estimate=pl.CostEstimate(
            flops=8 * units * arrivals * features, bytes_accessed=9 * 1024 * 1024, transcendentals=0
        ),
    )(saved_input, w_gate, gate_pair, w_up, up_pair, groups.T)
    down_part = pl.pallas_call(
        prepare_down_kernel,
        in_specs=[vmem, vmem, pl.BlockSpec(memory_space=pl.ANY)],
        out_shape=shape((chips, 2 * units, width), BF16),
        compiler_params=memory(6),
        cost_estimate=pl.CostEstimate(flops=0, bytes_accessed=4 * 1024 * 1024, transcendentals=0),
    )(w_down, down_pair, place)
    full = exchange(spread, "chip", plane)
    part = pl.pallas_call(
        down_kernel,
        out_shape=shape((2 * units, arrivals), F32),
        compiler_params=memory(6),
    )(full, down_part)
    pair = swap(part)
    term = pl.pallas_call(
        expert_kernel,
        out_shape=shape((chips, ROW_PAD, arrivals), BF16),
        compiler_params=memory(8),
    )(part, pair, pre, scale, back_part)
    terms = exchange(term, "chip", plane)
    back = pl.pallas_call(
        lambda *refs: return_kernel(width, *refs),
        out_shape=shape((rows, LANES), BF16),
        compiler_params=memory(6),
    )(terms)
    back = exchange(back.reshape(nodes, 2 * CAP, LANES), "node", ring_back).reshape(rows, LANES)
    in_grad, score = pl.pallas_call(
        combine_kernel,
        out_shape=(shape((tokens, width), BF16), shape((GROUP_MOST, tokens), F32)),
        compiler_params=memory(4),
    )(back, place)
    return in_grad, score.T


def solution(mesh):
    devices = mesh.devices
    split = jax.sharding.Mesh(
        devices.reshape(devices.shape[0], devices.shape[1] // 2, 2), ("node", "chip", "core")
    )
    local = ("chip", "core")
    every = ("node", "chip", "core")
    placed = (
        P("node", local),
        P("node", None),
        P("node", None),
        P("node", None),
        P(None, every),
        P(None, every),
        P(every, None),
    )
    return jax.shard_map(
        on_device,
        mesh=split,
        in_specs=placed,
        out_specs=(P("node", local), P("node", None)),
        check_vma=False,
    )
```

```python
import jax
import jax.numpy as jnp
from jax import lax
from jax.experimental import pallas as pl
from jax.experimental.pallas import tpu as pltpu
from jax.sharding import PartitionSpec as P

GROUP_MOST = 4
FIRST_OUT, FIRST_BACK = 22, 17
CAP = 4
LANES = 128
BF16 = jnp.bfloat16
F32 = jnp.float32
ROW_PAD = 240


def dot(a, b, contract):
    return lax.dot_general(
        a, b, ((contract[:1], contract[1:]), ((), ())), preferred_element_type=F32
    )


def iota(shape, dim):
    return lax.broadcasted_iota(jnp.int32, shape, dim)


def chip_at(position, chips):
    return (position + 7 * chips // 8) % chips


def node_at(position, nodes, first):
    return (position + first * nodes // 32) % nodes


def fetch(pairs, sems):
    copies = [pltpu.make_async_copy(src, dst, sems.at[i]) for i, (src, dst) in enumerate(pairs)]
    for copy in copies:
        copy.start()
    return copies


def placement(tokens, rows, first):
    row = iota((tokens, rows), 1)
    nodes = rows // (2 * CAP)
    node = node_at(row // (2 * CAP), nodes, first).astype(F32)
    half, slot = row // CAP % 2, (row % CAP).astype(F32)
    low, high = (half == 0).astype(F32), (half == 1).astype(F32)
    earlier = (iota((tokens, tokens), 1) < iota((tokens, tokens), 0)).astype(BF16)

    def of(columns):
        named = [(columns[:, i : i + 1] == node).astype(F32) for i in range(GROUP_MOST)]
        visits = named[0] + named[1] + named[2] + named[3]
        here = (dot(earlier, visits.astype(BF16), (1, 0)) == slot).astype(F32)
        return named, visits, here * low, here * high

    return of


def send_kernel(grad_hbm, groups_hbm, weight_hbm, send_ref, grad_ref, groups_ref, weight_ref, sems):
    tokens, width = grad_ref.shape
    rows = send_ref.shape[0]
    rest = width - LANES
    copies = fetch(
        [(groups_hbm, groups_ref), (weight_hbm, weight_ref), (grad_hbm, grad_ref)], sems
    )
    place = placement(tokens, rows, FIRST_OUT)
    same = (iota((tokens, tokens), 0) == iota((tokens, tokens), 1)).astype(BF16)
    marks = (iota((tokens, LANES), 1) == rest).astype(F32)
    copies[0].wait()
    copies[1].wait()
    both = jnp.concatenate([groups_ref[...].astype(F32), weight_ref[...]], axis=0)
    columns = dot(same, both.astype(BF16), (1, 1))
    named, visits, low, high = place(columns)
    scale = columns[:, GROUP_MOST : GROUP_MOST + 1] * named[0]
    for i in range(1, GROUP_MOST):
        scale = scale + columns[:, GROUP_MOST + i : GROUP_MOST + i + 1] * named[i]
    picks = jnp.concatenate([low * visits, high * visits, high * scale], axis=0).astype(BF16)
    copies[2].wait()
    grad = grad_ref[...].astype(F32)
    values = jnp.concatenate(
        [
            grad[:, :LANES],
            jnp.concatenate([grad[:, LANES:], jnp.zeros((tokens, LANES - rest), F32)], axis=1),
            marks,
        ],
        axis=0,
    ).astype(BF16)
    send_ref[...] = dot(picks, values, (0, 0)).astype(BF16)


def pick(half, rows, arrivals, first):
    row, arrival = iota((rows, arrivals), 0), iota((rows, arrivals), 1)
    node = node_at(row // (2 * CAP), rows // (2 * CAP), first)
    same = (node == arrival // CAP) & (row % CAP == arrival % CAP)
    return (same & (row // CAP % 2 == half)).astype(BF16)


def spread_kernel(recv_ref, spread_hbm, scale_ref, slab_ref, sems):
    rows = recv_ref.shape[0]
    width, arrivals = slab_ref.shape
    recv = recv_ref[...]
    low = dot(recv, pick(0, rows, arrivals, FIRST_OUT), (0, 0))
    high = dot(recv, pick(1, rows, arrivals, FIRST_OUT), (0, 0))
    rest = width - LANES
    scale_ref[...] = high[rest : rest + 1, :]
    slab_ref[...] = jnp.concatenate([low, high[:rest, :]], axis=0).astype(BF16)
    copies = fetch([(slab_ref, spread_hbm.at[i]) for i in range(spread_hbm.shape[0])], sems)
    for copy in copies:
        copy.wait()


def prepare_down_kernel(down_ref, down_pair_ref, prepared_ref, down_part_ref):
    units = down_ref.shape[0]
    chips, _, width = down_part_ref.shape
    core = lax.axis_index("core")
    for parity in range(2):

        @pl.when(core == parity)
        def _():
            for k in range(chips):
                first = (2 * chip_at(k, chips) + parity) * width
                down_part_ref[k, :units] = down_ref[:, first : first + width]
                down_part_ref[k, units:] = down_pair_ref[:, first : first + width]


def prepare_kernel(
    saved_hbm, gate_hbm, gate_pair_hbm, up_hbm, up_pair_hbm, groups_ref,
    pre_ref, back_part_ref, place_ref,
    saved_ref, weight_ref, sems,
):
    units = gate_hbm.shape[0]
    chips, width, _ = back_part_ref.shape
    copies = fetch(
        [
            (gate_hbm, weight_ref.at[pl.ds(0, units)]),
            (gate_pair_hbm, weight_ref.at[pl.ds(units, units)]),
            (up_hbm, weight_ref.at[pl.ds(2 * units, units)]),
            (up_pair_hbm, weight_ref.at[pl.ds(3 * units, units)]),
            (saved_hbm, saved_ref),
        ],
        sems,
    )
    tokens = groups_ref.shape[1]
    same = (iota((tokens, tokens), 0) == iota((tokens, tokens), 1)).astype(BF16)
    columns = dot(same, groups_ref[...].astype(F32).astype(BF16), (1, 1))
    named, _, low, high = placement(tokens, place_ref.shape[1], FIRST_BACK)(columns)
    parts = [part * named[i] for part in (low, high) for i in range(GROUP_MOST)]
    place_ref[...] = jnp.concatenate(parts, axis=0).astype(BF16)
    core = lax.axis_index("core")
    for copy in copies[:4]:
        copy.wait()
    for parity in range(2):

        @pl.when(core == parity)
        def _():
            for k in range(chips):
                first = (2 * chip_at(k, chips) + parity) * width
                back_part_ref[k] = weight_ref[:, first : first + width].T

    copies[4].wait()
    pre_ref[...] = dot(weight_ref[...], saved_ref[...], (1, 1))


def down_kernel(rows_ref, down_ref, part_ref):
    total = dot(down_ref[0], rows_ref[0], (1, 0))
    for k in range(1, rows_ref.shape[0]):
        total = total + dot(down_ref[k], rows_ref[k], (1, 0))
    part_ref[...] = total


def expert_kernel(part_ref, pair_ref, pre_ref, scale_ref, weight_ref, term_ref):
    units = part_ref.shape[0] // 2
    pair = pair_ref[...]
    down_grad = part_ref[...] + jnp.concatenate([pair[units:], pair[:units]], axis=0)
    gate_pre, up_pre = pre_ref[: 2 * units, :], pre_ref[2 * units :, :]
    sigmoid_gate = jax.nn.sigmoid(gate_pre)
    silu_value = gate_pre * sigmoid_gate
    score = jnp.sum(silu_value * up_pre * down_grad, axis=0, keepdims=True)
    hidden_grad = scale_ref[...] * down_grad
    gate_grad = hidden_grad * up_pre * sigmoid_gate * (1.0 + gate_pre * (1.0 - sigmoid_gate))
    up_grad = hidden_grad * silu_value
    grads = jnp.concatenate([gate_grad, up_grad], axis=0).astype(BF16)
    chips, padded, arrivals = term_ref.shape
    width = weight_ref.shape[1]
    score_high = score.astype(BF16).astype(F32)
    extra_row = iota((padded - width, arrivals), 0)
    extra = jnp.where(extra_row == 0, score_high, jnp.where(extra_row == 1, score - score_high, 0.0))
    extra = extra.astype(BF16)
    for k in range(chips):
        term_ref[k, :width, :] = dot(weight_ref[k], grads, (1, 0)).astype(BF16)
        term_ref[k, width:padded, :] = extra


def return_kernel(width, part_ref, back_ref):
    holders, padded, arrivals = part_ref.shape
    total = part_ref[0].astype(F32)
    for holder in range(1, holders):
        total = total + part_ref[holder].astype(F32)
    rows = back_ref.shape[0]
    score = total[width : width + 1, :] + total[width + 1 : width + 2, :]
    score_high = score.astype(BF16).astype(F32)
    extra_row = iota((2 * LANES - width, arrivals), 0)
    extra = jnp.where(extra_row == 0, score_high, jnp.where(extra_row == 1, score - score_high, 0.0))
    low = total[:LANES].astype(BF16)
    high = jnp.concatenate([total[LANES:width], extra], axis=0).astype(BF16)
    back = dot(pick(0, rows, arrivals, FIRST_BACK), low, (1, 1))
    back = back + dot(pick(1, rows, arrivals, FIRST_BACK), high, (1, 1))
    back_ref[...] = back.astype(BF16)


def combine_kernel(back_ref, place_ref, grad_ref, score_ref):
    tokens, width = grad_ref.shape
    rest = width - LANES
    back, place = back_ref[...], place_ref[...]
    sums = dot(place, back, (1, 0))
    low = sums[0:tokens]
    high = sums[GROUP_MOST * tokens : (GROUP_MOST + 1) * tokens]
    for i in range(1, GROUP_MOST):
        low = low + sums[i * tokens : (i + 1) * tokens]
        high = high + sums[(GROUP_MOST + i) * tokens : (GROUP_MOST + i + 1) * tokens]
    grad_ref[:, :LANES] = low.astype(BF16)
    grad_ref[:, LANES:] = high[:, :rest].astype(BF16)
    lane = iota((16, LANES), 1)
    chosen = (lane == rest + iota((16, LANES), 0)) & (iota((16, LANES), 0) < 2)
    scores = dot(chosen.astype(BF16), back, (1, 1)).astype(BF16)
    values = dot(scores, place, (1, 1))
    values = values[0:1] + values[1:2]
    for i in range(GROUP_MOST):
        first = (GROUP_MOST + i) * tokens
        score_ref[i : i + 1, :] = values[:, first : first + tokens]


def shape(dims, dtype):
    return jax.ShapeDtypeStruct(dims, dtype)


def exchange(x, axis, groups=None):
    return lax.all_to_all(
        x, axis, split_axis=0, concat_axis=0, tiled=True, axis_index_groups=groups
    )


def memory(mebibytes):
    return pltpu.CompilerParams(vmem_limit_bytes=mebibytes * 1024 * 1024)


def swap(x):
    return lax.ppermute(x, "core", [(0, 1), (1, 0)])


def on_device(out_grad, groups, route_weight, saved_input, w_gate, w_up, w_down):
    tokens, width = out_grad.shape
    nodes, chips = lax.axis_size("node"), lax.axis_size("chip")
    rows, arrivals, units = nodes * 2 * CAP, nodes * CAP, w_down.shape[0]
    ring_out = [[node_at(i, nodes, FIRST_OUT) for i in range(nodes)]]
    ring_back = [[node_at(i, nodes, FIRST_BACK) for i in range(nodes)]]
    plane = [[chip_at(i, chips) for i in range(chips)]]
    hbm, vmem = pl.BlockSpec(memory_space=pltpu.HBM), pl.BlockSpec(memory_space=pltpu.VMEM)
    send = pl.pallas_call(
        send_kernel,
        in_specs=[hbm] * 3,
        out_shape=shape((rows, LANES), BF16),
        scratch_shapes=[
            pltpu.VMEM((tokens, width), BF16),
            pltpu.VMEM((GROUP_MOST, tokens), jnp.int32),
            pltpu.VMEM((GROUP_MOST, tokens), F32),
            pltpu.SemaphoreType.DMA((3,)),
        ],
    )(out_grad, groups.T, route_weight.T)
    w_gate, w_up = w_gate.T, w_up.T
    gate_pair, up_pair, down_pair = swap(w_gate), swap(w_up), swap(w_down)
    recv = exchange(send.reshape(nodes, 2 * CAP, LANES), "node", ring_out).reshape(rows, LANES)
    spread, scale = pl.pallas_call(
        spread_kernel,
        out_specs=(hbm, vmem),
        out_shape=(shape((chips, width, arrivals), BF16), shape((1, arrivals), F32)),
        scratch_shapes=[pltpu.VMEM((width, arrivals), BF16), pltpu.SemaphoreType.DMA((chips,))],
        compiler_params=memory(6),
    )(recv)
    features = saved_input.shape[1]
    pre, back_part, place = pl.pallas_call(
        prepare_kernel,
        in_specs=[hbm] * 5 + [vmem],
        out_shape=(
            shape((4 * units, arrivals), F32),
            shape((chips, width, 4 * units), BF16),
            shape((2 * GROUP_MOST * tokens, rows), BF16),
        ),
        scratch_shapes=[
            pltpu.VMEM((arrivals, features), BF16),
            pltpu.VMEM((4 * units, features), BF16),
            pltpu.SemaphoreType.DMA((5,)),
        ],
        compiler_params=memory(60),
        cost_estimate=pl.CostEstimate(
            flops=8 * units * arrivals * features, bytes_accessed=9 * 1024 * 1024, transcendentals=0
        ),
    )(saved_input, w_gate, gate_pair, w_up, up_pair, groups.T)
    down_part = pl.pallas_call(
        prepare_down_kernel,
        in_specs=[vmem, vmem, pl.BlockSpec(memory_space=pl.ANY)],
        out_shape=shape((chips, 2 * units, width), BF16),
        compiler_params=memory(6),
        cost_estimate=pl.CostEstimate(flops=0, bytes_accessed=4 * 1024 * 1024, transcendentals=0),
    )(w_down, down_pair, place)
    full = exchange(spread, "chip", plane)
    part = pl.pallas_call(
        down_kernel,
        out_shape=shape((2 * units, arrivals), F32),
        compiler_params=memory(6),
    )(full, down_part)
    pair = swap(part)
    term = pl.pallas_call(
        expert_kernel,
        out_shape=shape((chips, ROW_PAD, arrivals), BF16),
        compiler_params=memory(8),
    )(part, pair, pre, scale, back_part)
    terms = exchange(term, "chip", plane)
    back = pl.pallas_call(
        lambda *refs: return_kernel(width, *refs),
        out_shape=shape((rows, LANES), BF16),
        compiler_params=memory(6),
    )(terms)
    back = exchange(back.reshape(nodes, 2 * CAP, LANES), "node", ring_back).reshape(rows, LANES)
    in_grad, score = pl.pallas_call(
        combine_kernel,
        out_shape=(shape((tokens, width), BF16), shape((GROUP_MOST, tokens), F32)),
        compiler_params=memory(4),
    )(back, place)
    return in_grad, score.T


def solution(mesh):
    devices = mesh.devices
    split = jax.sharding.Mesh(
        devices.reshape(devices.shape[0], devices.shape[1] // 2, 2), ("node", "chip", "core")
    )
    local = ("chip", "core")
    every = ("node", "chip", "core")
    placed = (
        P("node", local),
        P("node", None),
        P("node", None),
        P("node", None),
        P(None, every),
        P(None, every),
        P(every, None),
    )
    return jax.shard_map(
        on_device,
        mesh=split,
        in_specs=placed,
        out_specs=(P("node", local), P("node", None)),
        check_vma=False,
    )
```

```python
import jax
import jax.numpy as jnp
from jax import lax
from jax.experimental import pallas as pl
from jax.experimental.pallas import tpu as pltpu
from jax.sharding import PartitionSpec as P

GROUP_MOST = 4
FIRST_OUT, FIRST_BACK = 22, 17
CAP = 4
LANES = 128
BF16 = jnp.bfloat16
F32 = jnp.float32
ROW_PAD = 240


def dot(a, b, contract):
    return lax.dot_general(
        a, b, ((contract[:1], contract[1:]), ((), ())), preferred_element_type=F32
    )


def iota(shape, dim):
    return lax.broadcasted_iota(jnp.int32, shape, dim)


def chip_at(position, chips):
    return (position + 7 * chips // 8) % chips


def node_at(position, nodes, first):
    return (position + first * nodes // 32) % nodes


def fetch(pairs, sems):
    copies = [pltpu.make_async_copy(src, dst, sems.at[i]) for i, (src, dst) in enumerate(pairs)]
    for copy in copies:
        copy.start()
    return copies


def placement(tokens, rows, first):
    row = iota((tokens, rows), 1)
    nodes = rows // (2 * CAP)
    node = node_at(row // (2 * CAP), nodes, first).astype(F32)
    half, slot = row // CAP % 2, (row % CAP).astype(F32)
    low, high = (half == 0).astype(F32), (half == 1).astype(F32)
    earlier = (iota((tokens, tokens), 1) < iota((tokens, tokens), 0)).astype(BF16)

    def of(columns):
        named = [(columns[:, i : i + 1] == node).astype(F32) for i in range(GROUP_MOST)]
        visits = named[0] + named[1] + named[2] + named[3]
        here = (dot(earlier, visits.astype(BF16), (1, 0)) == slot).astype(F32)
        return named, visits, here * low, here * high

    return of


def send_kernel(grad_hbm, groups_hbm, weight_hbm, send_ref, grad_ref, groups_ref, weight_ref, sems):
    tokens, width = grad_ref.shape
    rows = send_ref.shape[0]
    rest = width - LANES
    copies = fetch(
        [(groups_hbm, groups_ref), (weight_hbm, weight_ref), (grad_hbm, grad_ref)], sems
    )
    place = placement(tokens, rows, FIRST_OUT)
    same = (iota((tokens, tokens), 0) == iota((tokens, tokens), 1)).astype(BF16)
    marks = (iota((tokens, LANES), 1) == rest).astype(F32)
    copies[0].wait()
    copies[1].wait()
    both = jnp.concatenate([groups_ref[...].astype(F32), weight_ref[...]], axis=0)
    columns = dot(same, both.astype(BF16), (1, 1))
    named, visits, low, high = place(columns)
    scale = columns[:, GROUP_MOST : GROUP_MOST + 1] * named[0]
    for i in range(1, GROUP_MOST):
        scale = scale + columns[:, GROUP_MOST + i : GROUP_MOST + i + 1] * named[i]
    picks = jnp.concatenate([low * visits, high * visits, high * scale], axis=0).astype(BF16)
    copies[2].wait()
    grad = grad_ref[...].astype(F32)
    values = jnp.concatenate(
        [
            grad[:, :LANES],
            jnp.concatenate([grad[:, LANES:], jnp.zeros((tokens, LANES - rest), F32)], axis=1),
            marks,
        ],
        axis=0,
    ).astype(BF16)
    send_ref[...] = dot(picks, values, (0, 0)).astype(BF16)


def pick(half, rows, arrivals, first):
    row, arrival = iota((rows, arrivals), 0), iota((rows, arrivals), 1)
    node = node_at(row // (2 * CAP), rows // (2 * CAP), first)
    same = (node == arrival // CAP) & (row % CAP == arrival % CAP)
    return (same & (row // CAP % 2 == half)).astype(BF16)


def spread_kernel(recv_ref, spread_hbm, scale_ref, slab_ref, sems):
    rows = recv_ref.shape[0]
    width, arrivals = slab_ref.shape
    recv = recv_ref[...]
    rest = width - LANES
    chips = spread_hbm.shape[0]
    slab_ref[:LANES, :] = dot(recv, pick(0, rows, arrivals, FIRST_OUT), (0, 0)).astype(BF16)
    first, last = pl.ds(0, LANES), pl.ds(LANES, rest)
    copies = fetch([(slab_ref.at[first], spread_hbm.at[i, first]) for i in range(chips)], sems.at[0])
    high = dot(recv, pick(1, rows, arrivals, FIRST_OUT), (0, 0))
    slab_ref[LANES:, :] = high[:rest, :].astype(BF16)
    copies += fetch([(slab_ref.at[last], spread_hbm.at[i, last]) for i in range(chips)], sems.at[1])
    scale_ref[...] = high[rest : rest + 1, :]
    for copy in copies:
        copy.wait()


def prepare_down_kernel(down_ref, down_pair_ref, prepared_ref, down_part_ref):
    units = down_ref.shape[0]
    chips, _, width = down_part_ref.shape
    core = lax.axis_index("core")
    for parity in range(2):

        @pl.when(core == parity)
        def _():
            for k in range(chips):
                first = (2 * chip_at(k, chips) + parity) * width
                down_part_ref[k, :units] = down_ref[:, first : first + width]
                down_part_ref[k, units:] = down_pair_ref[:, first : first + width]


def prepare_kernel(
    saved_hbm, gate_hbm, gate_pair_hbm, up_hbm, up_pair_hbm, groups_ref,
    pre_ref, back_part_ref, place_ref,
    saved_ref, weight_ref, sems,
):
    units = gate_hbm.shape[0]
    chips, width, _ = back_part_ref.shape
    copies = fetch(
        [
            (gate_hbm, weight_ref.at[pl.ds(0, units)]),
            (gate_pair_hbm, weight_ref.at[pl.ds(units, units)]),
            (up_hbm, weight_ref.at[pl.ds(2 * units, units)]),
            (up_pair_hbm, weight_ref.at[pl.ds(3 * units, units)]),
            (saved_hbm, saved_ref),
        ],
        sems,
    )
    tokens = groups_ref.shape[1]
    same = (iota((tokens, tokens), 0) == iota((tokens, tokens), 1)).astype(BF16)
    columns = dot(same, groups_ref[...].astype(F32).astype(BF16), (1, 1))
    named, _, low, high = placement(tokens, place_ref.shape[1], FIRST_BACK)(columns)
    parts = [part * named[i] for part in (low, high) for i in range(GROUP_MOST)]
    place_ref[...] = jnp.concatenate(parts, axis=0).astype(BF16)
    core = lax.axis_index("core")
    for copy in copies[:4]:
        copy.wait()
    for parity in range(2):

        @pl.when(core == parity)
        def _():
            for k in range(chips):
                first = (2 * chip_at(k, chips) + parity) * width
                back_part_ref[k] = weight_ref[:, first : first + width].T

    copies[4].wait()
    pre_ref[...] = dot(weight_ref[...], saved_ref[...], (1, 1))


def down_kernel(rows_ref, down_ref, part_ref):
    total = dot(down_ref[0], rows_ref[0], (1, 0))
    for k in range(1, rows_ref.shape[0]):
        total = total + dot(down_ref[k], rows_ref[k], (1, 0))
    part_ref[...] = total


def expert_kernel(part_ref, pair_ref, pre_ref, scale_ref, weight_ref, term_ref):
    units = part_ref.shape[0] // 2
    pair = pair_ref[...]
    down_grad = part_ref[...] + jnp.concatenate([pair[units:], pair[:units]], axis=0)
    gate_pre, up_pre = pre_ref[: 2 * units, :], pre_ref[2 * units :, :]
    sigmoid_gate = jax.nn.sigmoid(gate_pre)
    silu_value = gate_pre * sigmoid_gate
    score = jnp.sum(silu_value * up_pre * down_grad, axis=0, keepdims=True)
    hidden_grad = scale_ref[...] * down_grad
    gate_grad = hidden_grad * up_pre * sigmoid_gate * (1.0 + gate_pre * (1.0 - sigmoid_gate))
    up_grad = hidden_grad * silu_value
    grads = jnp.concatenate([gate_grad, up_grad], axis=0).astype(BF16)
    chips, padded, arrivals = term_ref.shape
    width = weight_ref.shape[1]
    score_high = score.astype(BF16).astype(F32)
    extra_row = iota((padded - width, arrivals), 0)
    extra = jnp.where(extra_row == 0, score_high, jnp.where(extra_row == 1, score - score_high, 0.0))
    extra = extra.astype(BF16)
    for k in range(chips):
        term_ref[k, :width, :] = dot(weight_ref[k], grads, (1, 0)).astype(BF16)
        term_ref[k, width:padded, :] = extra


def return_kernel(width, part_ref, back_ref):
    holders, padded, arrivals = part_ref.shape
    total = part_ref[0].astype(F32)
    for holder in range(1, holders):
        total = total + part_ref[holder].astype(F32)
    rows = back_ref.shape[0]
    score = total[width : width + 1, :] + total[width + 1 : width + 2, :]
    score_high = score.astype(BF16).astype(F32)
    extra_row = iota((2 * LANES - width, arrivals), 0)
    extra = jnp.where(extra_row == 0, score_high, jnp.where(extra_row == 1, score - score_high, 0.0))
    low = total[:LANES].astype(BF16)
    high = jnp.concatenate([total[LANES:width], extra], axis=0).astype(BF16)
    back = dot(pick(0, rows, arrivals, FIRST_BACK), low, (1, 1))
    back = back + dot(pick(1, rows, arrivals, FIRST_BACK), high, (1, 1))
    back_ref[...] = back.astype(BF16)


def combine_kernel(back_ref, place_ref, grad_ref, score_ref):
    tokens, width = grad_ref.shape
    rest = width - LANES
    back, place = back_ref[...], place_ref[...]
    sums = dot(place, back, (1, 0))
    low = sums[0:tokens]
    high = sums[GROUP_MOST * tokens : (GROUP_MOST + 1) * tokens]
    for i in range(1, GROUP_MOST):
        low = low + sums[i * tokens : (i + 1) * tokens]
        high = high + sums[(GROUP_MOST + i) * tokens : (GROUP_MOST + i + 1) * tokens]
    grad_ref[:, :LANES] = low.astype(BF16)
    grad_ref[:, LANES:] = high[:, :rest].astype(BF16)
    lane = iota((16, LANES), 1)
    chosen = (lane == rest + iota((16, LANES), 0)) & (iota((16, LANES), 0) < 2)
    scores = dot(chosen.astype(BF16), back, (1, 1)).astype(BF16)
    values = dot(scores, place, (1, 1))
    values = values[0:1] + values[1:2]
    for i in range(GROUP_MOST):
        first = (GROUP_MOST + i) * tokens
        score_ref[i : i + 1, :] = values[:, first : first + tokens]


def shape(dims, dtype):
    return jax.ShapeDtypeStruct(dims, dtype)


def exchange(x, axis, groups=None):
    return lax.all_to_all(
        x, axis, split_axis=0, concat_axis=0, tiled=True, axis_index_groups=groups
    )


def memory(mebibytes):
    return pltpu.CompilerParams(vmem_limit_bytes=mebibytes * 1024 * 1024)


def swap(x):
    return lax.ppermute(x, "core", [(0, 1), (1, 0)])


def on_device(out_grad, groups, route_weight, saved_input, w_gate, w_up, w_down):
    tokens, width = out_grad.shape
    nodes, chips = lax.axis_size("node"), lax.axis_size("chip")
    rows, arrivals, units = nodes * 2 * CAP, nodes * CAP, w_down.shape[0]
    ring_out = [[node_at(i, nodes, FIRST_OUT) for i in range(nodes)]]
    ring_back = [[node_at(i, nodes, FIRST_BACK) for i in range(nodes)]]
    plane = [[chip_at(i, chips) for i in range(chips)]]
    hbm, vmem = pl.BlockSpec(memory_space=pltpu.HBM), pl.BlockSpec(memory_space=pltpu.VMEM)
    send = pl.pallas_call(
        send_kernel,
        in_specs=[hbm] * 3,
        out_shape=shape((rows, LANES), BF16),
        scratch_shapes=[
            pltpu.VMEM((tokens, width), BF16),
            pltpu.VMEM((GROUP_MOST, tokens), jnp.int32),
            pltpu.VMEM((GROUP_MOST, tokens), F32),
            pltpu.SemaphoreType.DMA((3,)),
        ],
    )(out_grad, groups.T, route_weight.T)
    w_gate, w_up = w_gate.T, w_up.T
    gate_pair, up_pair, down_pair = swap(w_gate), swap(w_up), swap(w_down)
    recv = exchange(send.reshape(nodes, 2 * CAP, LANES), "node", ring_out).reshape(rows, LANES)
    spread, scale = pl.pallas_call(
        spread_kernel,
        out_specs=(hbm, vmem),
        out_shape=(shape((chips, width, arrivals), BF16), shape((1, arrivals), F32)),
        scratch_shapes=[pltpu.VMEM((width, arrivals), BF16), pltpu.SemaphoreType.DMA((2, chips))],
        compiler_params=memory(6),
    )(recv)
    features = saved_input.shape[1]
    pre, back_part, place = pl.pallas_call(
        prepare_kernel,
        in_specs=[hbm] * 5 + [vmem],
        out_shape=(
            shape((4 * units, arrivals), F32),
            shape((chips, width, 4 * units), BF16),
            shape((2 * GROUP_MOST * tokens, rows), BF16),
        ),
        scratch_shapes=[
            pltpu.VMEM((arrivals, features), BF16),
            pltpu.VMEM((4 * units, features), BF16),
            pltpu.SemaphoreType.DMA((5,)),
        ],
        compiler_params=memory(60),
        cost_estimate=pl.CostEstimate(
            flops=8 * units * arrivals * features, bytes_accessed=9 * 1024 * 1024, transcendentals=0
        ),
    )(saved_input, w_gate, gate_pair, w_up, up_pair, groups.T)
    down_part = pl.pallas_call(
        prepare_down_kernel,
        in_specs=[vmem, vmem, pl.BlockSpec(memory_space=pl.ANY)],
        out_shape=shape((chips, 2 * units, width), BF16),
        compiler_params=memory(6),
        cost_estimate=pl.CostEstimate(flops=0, bytes_accessed=4 * 1024 * 1024, transcendentals=0),
    )(w_down, down_pair, place)
    full = exchange(spread, "chip", plane)
    part = pl.pallas_call(
        down_kernel,
        out_shape=shape((2 * units, arrivals), F32),
        compiler_params=memory(6),
    )(full, down_part)
    pair = swap(part)
    term = pl.pallas_call(
        expert_kernel,
        out_shape=shape((chips, ROW_PAD, arrivals), BF16),
        compiler_params=memory(8),
    )(part, pair, pre, scale, back_part)
    terms = exchange(term, "chip", plane)
    back = pl.pallas_call(
        lambda *refs: return_kernel(width, *refs),
        out_shape=shape((rows, LANES), BF16),
        compiler_params=memory(6),
    )(terms)
    back = exchange(back.reshape(nodes, 2 * CAP, LANES), "node", ring_back).reshape(rows, LANES)
    in_grad, score = pl.pallas_call(
        combine_kernel,
        out_shape=(shape((tokens, width), BF16), shape((GROUP_MOST, tokens), F32)),
        compiler_params=memory(4),
    )(back, place)
    return in_grad, score.T


def solution(mesh):
    devices = mesh.devices
    split = jax.sharding.Mesh(
        devices.reshape(devices.shape[0], devices.shape[1] // 2, 2), ("node", "chip", "core")
    )
    local = ("chip", "core")
    every = ("node", "chip", "core")
    placed = (
        P("node", local),
        P("node", None),
        P("node", None),
        P("node", None),
        P(None, every),
        P(None, every),
        P(every, None),
    )
    return jax.shard_map(
        on_device,
        mesh=split,
        in_specs=placed,
        out_specs=(P("node", local), P("node", None)),
        check_vma=False,
    )
```
